32 devices in a mesh: group: 2 (over y), dp: 4 (over x, core), mp: 4 (over z).
Axes of the slice: x: 2, y: 2, z: 4, core: 2. Of those that a mesh axis runs over, the one named last changes fastest.
Arguments:
- values: bfloat16 [8, 4, 128, 4096], P(('group', 'dp'), 'mp'), parts along dimension 0, may hold values from -0.25 to 0.25
- rows: int32 [8, 4, 128], P(('group', 'dp'), 'mp'), parts along dimension 0, may hold values from 0 to 31, as said below
- cols: int32 [8, 4, 128], P(('group', 'dp'), 'mp'), parts along dimension 0, may hold values from 0 to 31
- counts: int32 [8, 4], P(('group', 'dp'), 'mp'), parts along dimension 0, may hold values from 32 to 128, as said below
- weights: float32 [16384], P(('group', 'dp')), parts along dimension 0, may hold values from 0.2 to 5
- probes: bfloat16 [256, 64, 64], P(('group', 'mp'), 'dp'), parts along dimension 0, may hold values from -6 to 6
Outputs:
- sketch: float32 [256, 64, 64], P(('group', 'mp'), 'dp'), parts along dimension 0
The draws below stay inside these ranges and needn't reach their ends.
There are 2 independent parts, one for each index of `group`. The reference program is written for one: setup_inputs(seed, part) draws one part's arguments, and reference() takes and returns one part's arrays. A program takes and returns all parts, laid end to end along the dimension named above; each array names one. Nothing has to cross between parts.
Inputs may be any that keep to these rules, and one draw needn't show every extreme that they name: Within one device the pairs (rows, cols) of its 128 slots are all distinct. `counts`: the live slots of a device are its first ones; some device has all 128 live.
All inputs are finite; a program needn't handle non-finite values.
Results may differ from the reference program's by a relative error of at most 0.0023.
Values may be sent and summed in bfloat16 or wider, within the bound.
A program may use at most 64 MiB of HBM per device.

```python
import math
import jax
import jax.numpy as jnp
from jax import lax

BS = 64
P_SIZE = 64
DB_DEV = 32
CB_DEV = 32
NB_CAP = 128
NDATA = 8192
NCB = 128
N_DP = 4
N_MP = 4


def tile_positions(key):
    keys = jax.random.split(key, N_DP * N_MP)
    picked = jax.vmap(lambda k: jax.random.permutation(k, DB_DEV * CB_DEV)[:NB_CAP])(keys)
    return picked.reshape(N_DP, N_MP, NB_CAP).astype(jnp.int32)


def draw_rows(key, part):
    return tile_positions(key) // CB_DEV


def draw_cols(key, part):
    return tile_positions(key) % CB_DEV


def draw_counts(key, part):
    key = jax.random.fold_in(key, 5)
    first, second = jax.random.split(key, 2)
    total = N_DP * N_MP
    divisor = jax.random.randint(first, (total,), 1, 5)
    live = NB_CAP // divisor
    busiest = jax.random.randint(second, (), 0, total)
    live = live.at[busiest].set(NB_CAP)
    live = live.at[(busiest + 1) % total].set(NB_CAP // 4)
    return live.reshape(N_DP, N_MP).astype(jnp.int32)


def steps_of(rng, shape, cuts, low, top_value):
    def one(dim, blocks):
        steps = jax.random.uniform(jax.random.fold_in(jax.random.fold_in(rng, 6), dim), (blocks,), jnp.float32, low / len(cuts), top_value / len(cuts))
        return jnp.repeat(jnp.exp(steps), shape[dim] // blocks).reshape((-1,) + (1,) * (len(shape) - dim - 1))

    factor_of = one(*cuts[0])
    for cut in cuts[1:]:
        factor_of = factor_of * one(*cut)
    return factor_of


def noise(rng, shape, deviation, limit, cuts=(), kind=jnp.bfloat16):
    factor_of = steps_of(rng, shape, cuts, -0.22, 0.18) if cuts else 1.0
    array = jax.random.normal(rng, shape, jnp.float32) * deviation * factor_of
    return jnp.minimum(jnp.maximum(array, -limit), limit).astype(kind)


def setup_inputs(seed: int = 0, part: int = 0) -> dict:
    splits = jax.random.split(jax.random.key(seed), 7)
    part_splits = jax.random.split(jax.random.fold_in(splits[6], part), 7)
    return {
        "values": noise(part_splits[0], (N_DP, N_MP, NB_CAP, BS * BS), (NB_CAP * N_MP * BS // (2 * DB_DEV)) ** -0.5, 0.25, ((0, 4), (1, 4))),
        "rows": draw_rows(jax.random.fold_in(jax.random.fold_in(splits[6], part), 71), part),
        "cols": draw_cols(jax.random.fold_in(jax.random.fold_in(splits[6], part), 71), part),
        "counts": draw_counts(jax.random.fold_in(jax.random.fold_in(splits[6], part), 71), part),
        "weights": jnp.clip(jnp.exp(math.log(5.0) - 3.218876 * jax.random.uniform(part_splits[4], (NDATA,), jnp.float32) ** steps_of(part_splits[4], (NDATA,), ((0, 4),), -0.2, 0.2)), 0.2, 5.0),
        "probes": noise(part_splits[5], (NCB, BS, P_SIZE), 1.0, 6.0, ((0, 4), (1, 4))),
    }


def reference(values, rows, cols, counts, weights, probes):
    panels = probes.reshape(N_MP, CB_DEV, BS, P_SIZE)
    slots = jnp.arange(NB_CAP, dtype=jnp.int32)

    def block_values(i, j):
        live = slots < counts[i, j]
        square = values[i, j].reshape(NB_CAP, BS, BS).astype(jnp.float32)
        return jnp.where(live[:, None, None], square, 0.0)

    def per_data(i):
        def step(total, j):
            chosen = panels[j][cols[i, j]].astype(jnp.float32)
            prod = jnp.einsum("bij,bjp->bip", block_values(i, j), chosen, precision=lax.Precision.HIGHEST)
            return total + jax.ops.segment_sum(prod, rows[i, j], num_segments=DB_DEV), None
        total, unused = lax.scan(step, jnp.zeros((DB_DEV, BS, P_SIZE), jnp.float32), jnp.arange(N_MP, dtype=jnp.int32))
        return total

    predicted = lax.map(per_data, jnp.arange(N_DP, dtype=jnp.int32))
    weighted = (weights.reshape(N_DP, DB_DEV, BS, 1) * predicted).astype(jnp.bfloat16)

    def per_cells(j):
        def step(total, i):
            chosen = weighted[i][rows[i, j]].astype(jnp.float32)
            prod = jnp.einsum("bij,bip->bjp", block_values(i, j), chosen, precision=lax.Precision.HIGHEST)
            return total + jax.ops.segment_sum(prod, cols[i, j], num_segments=CB_DEV), None
        total, unused = lax.scan(step, jnp.zeros((CB_DEV, BS, P_SIZE), jnp.float32), jnp.arange(N_DP, dtype=jnp.int32))
        return total

    sketch = lax.map(per_cells, jnp.arange(N_MP, dtype=jnp.int32))
    return sketch.reshape(N_MP * CB_DEV, BS, P_SIZE)
```

```python
import functools

import jax
import jax.numpy as jnp
from jax import lax
from jax.experimental import pallas as pl
from jax.experimental.pallas import tpu as pltpu
from jax.sharding import PartitionSpec as P

BS = 64
MESH = pl.DeviceIdType.MESH
BF16 = jnp.bfloat16
F32 = jnp.float32
PRED = jnp.float32


def both_halves(x):
    low, high = x[:, :BS], x[:, BS:]
    return jnp.concatenate([low, low], axis=1), jnp.concatenate([high, high], axis=1)


def kernel(n_dp, n_mp, n_data, n_cells,
           table, fwd_blocks, bwd_blocks, probes, weights, out,
           gathered, wide_f32, wide, fwd, bwd, psend, precv, own_pred, wgather, wide_w,
           ssend, srecv, own_sketch,
           gs, gr, ps, pr, ws, wr, ss, sr):
    dp, mp = lax.axis_index("dp"), lax.axis_index("mp")
    share = BS // n_dp
    owned = n_data // n_mp
    pairs = owned // 2
    half_cells = n_cells // 2
    side = lax.broadcasted_iota(jnp.int32, (BS, 2 * BS), 1) < BS

    barrier = pltpu.get_barrier_semaphore()
    for off in range(1, n_dp):
        pl.semaphore_signal(barrier, inc=1, device_id={"dp": lax.rem(dp + off, n_dp)}, device_id_type=MESH)
    for off in range(1, n_mp):
        pl.semaphore_signal(barrier, inc=1, device_id={"mp": lax.rem(mp + off, n_mp)}, device_id_type=MESH)
    pl.semaphore_wait(barrier, n_dp + n_mp - 2)

    def remote(src, dst, send, recv, axis, peer):
        return pltpu.make_async_remote_copy(
            src_ref=src, dst_ref=dst, send_sem=send, recv_sem=recv,
            device_id={axis: peer}, device_id_type=MESH)

    for off in range(1, n_dp):
        remote(probes, gathered.at[off - 1], gs.at[off - 1], gr.at[off - 1],
               "dp", lax.rem(dp + off, n_dp)).start()

    def build(blocks, strips, count, first, second):
        def one(block, carry):
            base = pl.multiple_of(block * BS, BS)
            for k in range(count // 2):
                a = blocks[table[block * first + (2 * k) * second]]
                b = blocks[table[block * first + (2 * k + 1) * second]]
                strips[pl.ds(base, BS), 2 * k * BS:(2 * k + 2) * BS] = jnp.where(side, a, b)
            return carry
        return one

    lax.fori_loop(0, n_data, build(fwd_blocks, fwd, n_cells, n_cells, 1), 0)

    def place(source, d):
        rows = source.astype(F32)
        start = pl.multiple_of(d * share, share)
        for c in range(half_cells):
            wide_f32[c, pl.ds(start, share), :] = rows[c * share:(c + 1) * share]

    place(probes[...], dp)
    for off in range(1, n_dp):
        remote(probes, gathered.at[off - 1], gs.at[off - 1], gr.at[off - 1], "dp", dp).wait_recv()
        place(gathered[off - 1], lax.rem(dp + n_dp - off, n_dp))
    for c in range(half_cells):
        low, high = both_halves(wide_f32[c])
        wide[c * BS:(c + 1) * BS] = low.astype(BF16)
        wide[(half_cells + c) * BS:(half_cells + c + 1) * BS] = high.astype(BF16)

    half = lax.broadcasted_iota(jnp.int32, (pairs * BS, 2 * BS), 1) < BS

    def predict(peer):
        start = pl.multiple_of(peer * (owned * BS), owned * BS)
        full = jnp.dot(fwd[pl.ds(start, owned * BS), :], wide[...], preferred_element_type=F32)
        return jnp.where(half, full[:pairs * BS], full[pairs * BS:])

    for off in range(1, n_mp):
        peer = lax.rem(mp + off, n_mp)
        psend[off - 1] = predict(peer).astype(PRED)
        remote(psend.at[off - 1], precv.at[off - 1], ps.at[off - 1], pr.at[off - 1], "mp", peer).start()
    own_pred[...] = predict(mp)

    lax.fori_loop(0, n_cells, build(bwd_blocks, bwd, n_data, 1, n_cells), 0)

    total = own_pred[...]
    for off in range(1, n_mp):
        remote(psend.at[off - 1], precv.at[off - 1], ps.at[off - 1], pr.at[off - 1], "mp", mp).wait_recv()
        total = total + precv[off - 1].astype(F32)
    wgather[0] = (weights[...] * total).astype(BF16)
    for off in range(1, n_mp):
        remote(wgather.at[0], wgather.at[off], ws.at[off - 1], wr.at[off - 1],
               "mp", lax.rem(mp + off, n_mp)).start()

    def place_w(source, k):
        low, high = both_halves(source.astype(F32))
        start = pl.multiple_of(k * (owned * BS), pairs * BS)
        wide_w[pl.ds(start, pairs * BS), :] = low.astype(BF16)
        wide_w[pl.ds(start + pairs * BS, pairs * BS), :] = high.astype(BF16)

    place_w(wgather[0], mp)
    for off in range(1, n_mp):
        remote(wgather.at[0], wgather.at[off], ws.at[off - 1], wr.at[off - 1], "mp", mp).wait_recv()
        place_w(wgather[off], lax.rem(mp + n_mp - off, n_mp))

    group = 8
    gp = group // 2
    half_g = lax.broadcasted_iota(jnp.int32, (gp * BS, 2 * BS), 1) < BS
    rows = gp * share
    for g in range(n_cells // group):
        full = jnp.dot(bwd[g * group * BS:(g + 1) * group * BS, :], wide_w[...], preferred_element_type=F32)
        packed = jnp.where(half_g, full[:gp * BS], full[gp * BS:])
        for d in range(n_dp):
            part = jnp.concatenate(
                [packed[p * BS + d * share:p * BS + (d + 1) * share] for p in range(gp)], axis=0)
            ssend[d, g * rows:(g + 1) * rows] = part.astype(BF16)

            @pl.when(dp == d)
            def _():
                own_sketch[g * rows:(g + 1) * rows] = part
        for off in range(1, n_dp):
            peer = lax.rem(dp + off, n_dp)
            remote(ssend.at[peer, pl.ds(g * rows, rows)], srecv.at[off - 1, pl.ds(g * rows, rows)],
                   ss.at[off - 1, g], sr.at[off - 1, g], "dp", peer).start()
    for g in range(n_cells // group):
        acc = own_sketch[g * rows:(g + 1) * rows]
        for off in range(1, n_dp):
            remote(ssend.at[0, pl.ds(g * rows, rows)], srecv.at[off - 1, pl.ds(g * rows, rows)],
                   ss.at[off - 1, g], sr.at[off - 1, g], "dp", dp).wait_recv()
            acc = acc + srecv[off - 1, g * rows:(g + 1) * rows].astype(F32)
        for p in range(gp):
            one = acc[p * share:(p + 1) * share]
            out[g * group + p] = one[:, :BS]
            out[g * group + gp + p] = one[:, BS:]

    for off in range(1, n_dp):
        remote(probes, gathered.at[off - 1], gs.at[off - 1], gr.at[off - 1], "dp", dp).wait_send()
        for g in range(n_cells // group):
            remote(ssend.at[0, pl.ds(g * rows, rows)], srecv.at[off - 1, pl.ds(g * rows, rows)],
                   ss.at[off - 1, g], sr.at[off - 1, g], "dp", dp).wait_send()
    for off in range(1, n_mp):
        remote(psend.at[off - 1], precv.at[off - 1], ps.at[off - 1], pr.at[off - 1], "mp", mp).wait_send()
        remote(wgather.at[0], wgather.at[off], ws.at[off - 1], wr.at[off - 1], "mp", mp).wait_send()


def body(n_dp, n_mp, values, rows, cols, counts, weights, probes):
    slots = values.shape[2]
    blocks = values[0, 0].reshape(slots, BS, BS)
    n_cells = probes.shape[0]
    share = probes.shape[1]
    n_data = weights.shape[0] // BS
    owned = n_data // n_mp
    pairs = owned // 2
    half_cells = n_cells // 2
    groups = n_cells // 8
    srows = 4 * share

    live = jnp.arange(slots, dtype=jnp.int32) < counts[0, 0]
    where = jnp.where(live, rows[0, 0] * n_cells + cols[0, 0], -1)
    places = jnp.arange(n_data * n_cells, dtype=jnp.int32)
    hit = places[:, None] == where[None, :]
    table = jnp.min(jnp.where(hit, jnp.arange(slots, dtype=jnp.int32)[None, :], slots), axis=1)

    blank = jnp.zeros((1, BS, 2 * BS), BF16)
    fwd_blocks = jnp.concatenate([jnp.concatenate([blocks, blocks], axis=2), blank], axis=0)
    turned = blocks.transpose(0, 2, 1)
    bwd_blocks = jnp.concatenate([jnp.concatenate([turned, turned], axis=2), blank], axis=0)
    packed = jnp.concatenate([probes[:half_cells], probes[half_cells:]], axis=2)
    packed = packed.reshape(half_cells * share, 2 * BS)
    mine = lax.dynamic_slice_in_dim(weights, lax.axis_index("mp") * (owned * BS), owned * BS)
    mine = mine.reshape(2, pairs * BS, 1)
    mine = jnp.concatenate(
        [jnp.broadcast_to(mine[0], (pairs * BS, BS)), jnp.broadcast_to(mine[1], (pairs * BS, BS))], axis=1)

    vmem = pl.BlockSpec(memory_space=pltpu.VMEM)
    dma = pltpu.SemaphoreType.DMA
    return pl.pallas_call(
        functools.partial(kernel, n_dp, n_mp, n_data, n_cells),
        out_shape=jax.ShapeDtypeStruct((n_cells, share, BS), F32),
        in_specs=[pl.BlockSpec(memory_space=pltpu.SMEM)] + [vmem] * 4,
        out_specs=vmem,
        scratch_shapes=[
            pltpu.VMEM((n_dp - 1, half_cells * share, 2 * BS), BF16),
            pltpu.VMEM((half_cells, BS, 2 * BS), F32),
            pltpu.VMEM((n_cells * BS, 2 * BS), BF16),
            pltpu.VMEM((n_data * BS, n_cells * BS), BF16),
            pltpu.VMEM((n_cells * BS, n_data * BS), BF16),
            pltpu.VMEM((n_mp - 1, pairs * BS, 2 * BS), PRED),
            pltpu.VMEM((n_mp - 1, pairs * BS, 2 * BS), PRED),
            pltpu.VMEM((pairs * BS, 2 * BS), F32),
            pltpu.VMEM((n_mp, pairs * BS, 2 * BS), BF16),
            pltpu.VMEM((n_data * BS, 2 * BS), BF16),
            pltpu.VMEM((n_dp, groups * srows, 2 * BS), BF16),
            pltpu.VMEM((n_dp - 1, groups * srows, 2 * BS), BF16),
            pltpu.VMEM((groups * srows, 2 * BS), F32),
            dma((n_dp - 1,)), dma((n_dp - 1,)),
            dma((n_mp - 1,)), dma((n_mp - 1,)),
            dma((n_mp - 1,)), dma((n_mp - 1,)),
            dma((n_dp - 1, groups)), dma((n_dp - 1, groups)),
        ],
        compiler_params=pltpu.CompilerParams(
            collective_id=0, has_side_effects=True, vmem_limit_bytes=48 * 1024 * 1024),
    )(table, fwd_blocks, bwd_blocks, packed, mine)


def solution(mesh):
    placed = (
        P(("group", "dp"), "mp", None, None),
        P(("group", "dp"), "mp", None),
        P(("group", "dp"), "mp", None),
        P(("group", "dp"), "mp"),
        P(("group", "dp")),
        P(("group", "mp"), "dp", None),
    )
    return jax.shard_map(
        functools.partial(body, mesh.shape["dp"], mesh.shape["mp"]),
        mesh=mesh, in_specs=placed, out_specs=P(("group", "mp"), "dp", None), check_vma=False
    )
```

```python
import functools

import jax
import jax.numpy as jnp
from jax import lax
from jax.experimental import pallas as pl
from jax.experimental.pallas import tpu as pltpu
from jax.sharding import PartitionSpec as P

BS = 64
MESH = pl.DeviceIdType.MESH
BF16 = jnp.bfloat16
F32 = jnp.float32


def both_halves(x):
    low, high = x[:, :BS], x[:, BS:]
    return jnp.concatenate([low, low], axis=1), jnp.concatenate([high, high], axis=1)


def kernel(n_dp, n_mp, n_data, n_cells, slots,
           table, values, probes, weights, out,
           flat, plain, turned, packed, gathered, wide_f32, wide, strips, psend, precv, own_pred,
           wgather, total_back, ssend, srecv, own_sketch,
           gs, gr, ps, pr, ws, wr, ss, sr):
    dp, mp = lax.axis_index("dp"), lax.axis_index("mp")
    share = BS // n_dp
    owned = n_data // n_mp
    pairs = owned // 2
    depth = owned * BS
    half_cells = n_cells // 2
    hb = BS // 2
    side = lax.broadcasted_iota(jnp.int32, (hb, 2 * BS), 1) < BS

    barrier = pltpu.get_barrier_semaphore()
    for off in range(1, n_dp):
        pl.semaphore_signal(barrier, inc=1, device_id={"dp": lax.rem(dp + off, n_dp)}, device_id_type=MESH)
    for off in range(1, n_mp):
        pl.semaphore_signal(barrier, inc=1, device_id={"mp": lax.rem(mp + off, n_mp)}, device_id_type=MESH)

    for c in range(half_cells):
        flat[c * share:(c + 1) * share] = jnp.concatenate([probes[c], probes[half_cells + c]], axis=1).astype(F32)
    packed[...] = flat[0:half_cells * share].astype(BF16)
    pl.semaphore_wait(barrier, n_dp + n_mp - 2)

    def remote(src, dst, send, recv, axis, peer):
        return pltpu.make_async_remote_copy(
            src_ref=src, dst_ref=dst, send_sem=send, recv_sem=recv,
            device_id={axis: peer}, device_id_type=MESH)

    for off in range(1, n_dp):
        remote(packed, gathered.at[off - 1], gs.at[off - 1], gr.at[off - 1],
               "dp", lax.rem(dp + off, n_dp)).start()

    for q in range(hb):
        flat[pl.ds(q, slots, stride=hb), :] = values[:, q * 2 * BS:(q + 1) * 2 * BS].astype(F32)

    def turn(s, carry):
        start = pl.multiple_of(s * (8 * hb), 8 * hb)
        rows = flat[pl.ds(start, 8 * hb), :]
        plain[pl.ds(s * 8, 8)] = rows.astype(BF16).reshape(8, hb, 2 * BS)
        turned[pl.ds(s * 8, 8)] = pltpu.roll(rows, BS, 1).astype(BF16).reshape(8, hb, 2 * BS)
        return carry

    lax.fori_loop(0, slots // 8, turn, 0)
    plain[slots] = jnp.zeros((hb, 2 * BS), BF16)
    turned[slots] = jnp.zeros((hb, 2 * BS), BF16)

    def build(block, carry):
        base = pl.multiple_of(block * BS, BS)
        for k in range(n_cells // 2):
            a = table[block * n_cells + 2 * k]
            b = table[block * n_cells + 2 * k + 1]
            lanes = slice(2 * k * BS, (2 * k + 2) * BS)
            strips[pl.ds(base, hb), lanes] = jnp.where(side, plain[a], turned[b])
            strips[pl.ds(base + hb, hb), lanes] = jnp.where(side, turned[a], plain[b])
        return carry

    lax.fori_loop(0, n_data, build, 0)

    def place(source, d):
        rows = source.astype(F32)
        start = pl.multiple_of(d * share, share)
        for c in range(half_cells):
            wide_f32[c, pl.ds(start, share), :] = rows[c * share:(c + 1) * share]

    place(packed[...], dp)
    for off in range(1, n_dp):
        remote(packed, gathered.at[off - 1], gs.at[off - 1], gr.at[off - 1], "dp", dp).wait_recv()
        place(gathered[off - 1], lax.rem(dp + n_dp - off, n_dp))
    for c in range(half_cells):
        low, high = both_halves(wide_f32[c])
        wide[c * BS:(c + 1) * BS] = low.astype(BF16)
        wide[(half_cells + c) * BS:(half_cells + c + 1) * BS] = high.astype(BF16)

    half = lax.broadcasted_iota(jnp.int32, (pairs * BS, 2 * BS), 1) < BS

    def rows_of(k):
        return pl.ds(pl.multiple_of(k * depth, depth), depth)

    def predict(peer):
        full = jnp.dot(strips[rows_of(peer), :], wide[...], preferred_element_type=F32)
        return jnp.where(half, full[:pairs * BS], full[pairs * BS:])

    for off in range(1, n_mp):
        peer = lax.rem(mp + off, n_mp)
        psend[off - 1] = predict(peer)
        remote(psend.at[off - 1], precv.at[off - 1], ps.at[off - 1], pr.at[off - 1], "mp", peer).start()
    own_pred[...] = predict(mp)

    i0 = lax.broadcasted_iota(jnp.int32, (2 * BS, 2 * BS), 0)
    i1 = lax.broadcasted_iota(jnp.int32, (2 * BS, 2 * BS), 1)
    inner = lax.rem(i1, BS)
    origin = i1 - inner + 2 * lax.rem(inner, hb) + inner // hb
    order = (i0 == origin).astype(F32)
    mine = weights[:, pl.ds(pl.multiple_of(mp * depth, depth), depth)]
    sorted_w = jnp.concatenate(
        [jnp.dot(jnp.broadcast_to(mine[:, k * 2 * BS:(k + 1) * 2 * BS], (8, 2 * BS)), order,
                 precision=lax.Precision.HIGHEST, preferred_element_type=F32) for k in range(owned // 2)], axis=1)
    factor = jnp.concatenate(
        [jnp.broadcast_to(sorted_w[0:1, :pairs * BS], (BS, pairs * BS)),
         jnp.broadcast_to(sorted_w[0:1, pairs * BS:], (BS, pairs * BS))], axis=0)

    total = own_pred[...]
    for off in range(1, n_mp):
        remote(psend.at[off - 1], precv.at[off - 1], ps.at[off - 1], pr.at[off - 1], "mp", mp).wait_recv()
        total = total + precv[off - 1]
    wgather[0] = (factor * total.T).astype(BF16)
    for off in range(1, n_mp):
        remote(wgather.at[0], wgather.at[off], ws.at[off - 1], wr.at[off - 1],
               "mp", lax.rem(mp + off, n_mp)).start()

    group = 8
    gp = group // 2
    cols = group * BS
    rows = gp * share

    def part_of(slot, k, g):
        chunk = wgather[slot]
        left = jnp.concatenate([chunk[:BS], chunk[BS:]], axis=1)
        return jnp.dot(left, strips[rows_of(k), g * cols:(g + 1) * cols], preferred_element_type=F32)

    n_groups = n_cells // group
    for off in range(n_mp):
        if off:
            remote(wgather.at[0], wgather.at[off], ws.at[off - 1], wr.at[off - 1], "mp", mp).wait_recv()
        for g in range(n_groups):
            lanes = slice(g * cols, (g + 1) * cols)
            part = part_of(off, lax.rem(mp + n_mp - off, n_mp), g)
            if off:
                part = part + total_back[:, lanes]
            if off < n_mp - 1:
                total_back[:, lanes] = part
                continue
            both = jnp.concatenate([part[:, :gp * BS], part[:, gp * BS:]], axis=0).T
            for d in range(n_dp):
                piece = jnp.concatenate(
                    [both[p * BS + d * share:p * BS + (d + 1) * share] for p in range(gp)], axis=0)
                ssend[d, g * rows:(g + 1) * rows] = piece.astype(BF16)

                @pl.when(dp == d)
                def _():
                    own_sketch[g * rows:(g + 1) * rows] = piece
            for o in range(1, n_dp):
                peer = lax.rem(dp + o, n_dp)
                remote(ssend.at[peer, pl.ds(g * rows, rows)], srecv.at[o - 1, pl.ds(g * rows, rows)],
                       ss.at[o - 1, g], sr.at[o - 1, g], "dp", peer).start()

    for g in range(n_groups):
        acc = own_sketch[g * rows:(g + 1) * rows]
        for off in range(1, n_dp):
            remote(ssend.at[0, pl.ds(g * rows, rows)], srecv.at[off - 1, pl.ds(g * rows, rows)],
                   ss.at[off - 1, g], sr.at[off - 1, g], "dp", dp).wait_recv()
            acc = acc + srecv[off - 1, g * rows:(g + 1) * rows].astype(F32)
        for p in range(gp):
            one = acc[p * share:(p + 1) * share]
            out[g * group + p] = one[:, :BS]
            out[g * group + gp + p] = one[:, BS:]

    for off in range(1, n_dp):
        remote(packed, gathered.at[off - 1], gs.at[off - 1], gr.at[off - 1], "dp", dp).wait_send()
        for g in range(n_groups):
            remote(ssend.at[0, pl.ds(g * rows, rows)], srecv.at[off - 1, pl.ds(g * rows, rows)],
                   ss.at[off - 1, g], sr.at[off - 1, g], "dp", dp).wait_send()
    for off in range(1, n_mp):
        remote(psend.at[off - 1], precv.at[off - 1], ps.at[off - 1], pr.at[off - 1], "mp", mp).wait_send()
        remote(wgather.at[0], wgather.at[off], ws.at[off - 1], wr.at[off - 1], "mp", mp).wait_send()


def body(n_dp, n_mp, values, rows, cols, counts, weights, probes):
    slots = values.shape[2]
    n_cells = probes.shape[0]
    share = probes.shape[1]
    n_data = weights.shape[0] // BS
    owned = n_data // n_mp
    pairs = owned // 2
    half_cells = n_cells // 2
    groups = n_cells // 8
    srows = 4 * share

    live = jnp.arange(slots, dtype=jnp.int32) < counts[0, 0]
    where = jnp.where(live, rows[0, 0] * n_cells + cols[0, 0], -1)
    places = jnp.arange(n_data * n_cells, dtype=jnp.int32)
    hit = places[:, None] == where[None, :]
    table = jnp.min(jnp.where(hit, jnp.arange(slots, dtype=jnp.int32)[None, :], slots), axis=1)

    vmem = pl.BlockSpec(memory_space=pltpu.VMEM)
    dma = pltpu.SemaphoreType.DMA
    return pl.pallas_call(
        functools.partial(kernel, n_dp, n_mp, n_data, n_cells, slots),
        out_shape=jax.ShapeDtypeStruct((n_cells, share, BS), F32),
        in_specs=[pl.BlockSpec(memory_space=pltpu.SMEM)] + [vmem] * 3,
        out_specs=vmem,
        scratch_shapes=[
            pltpu.VMEM((slots * BS // 2, 2 * BS), F32),
            pltpu.VMEM((slots + 1, BS // 2, 2 * BS), BF16),
            pltpu.VMEM((slots + 1, BS // 2, 2 * BS), BF16),
            pltpu.VMEM((half_cells * share, 2 * BS), BF16),
            pltpu.VMEM((n_dp - 1, half_cells * share, 2 * BS), BF16),
            pltpu.VMEM((half_cells, BS, 2 * BS), F32),
            pltpu.VMEM((n_cells * BS, 2 * BS), BF16),
            pltpu.VMEM((n_data * BS, n_cells * BS), BF16),
            pltpu.VMEM((n_mp - 1, pairs * BS, 2 * BS), F32),
            pltpu.VMEM((n_mp - 1, pairs * BS, 2 * BS), F32),
            pltpu.VMEM((pairs * BS, 2 * BS), F32),
            pltpu.VMEM((n_mp, 2 * BS, pairs * BS), BF16),
            pltpu.VMEM((BS, n_cells * BS), F32),
            pltpu.VMEM((n_dp, groups * srows, 2 * BS), BF16),
            pltpu.VMEM((n_dp - 1, groups * srows, 2 * BS), BF16),
            pltpu.VMEM((groups * srows, 2 * BS), F32),
            dma((n_dp - 1,)), dma((n_dp - 1,)),
            dma((n_mp - 1,)), dma((n_mp - 1,)),
            dma((n_mp - 1,)), dma((n_mp - 1,)),
            dma((n_dp - 1, groups)), dma((n_dp - 1, groups)),
        ],
        compiler_params=pltpu.CompilerParams(
            collective_id=0, has_side_effects=True, vmem_limit_bytes=48 * 1024 * 1024),
    )(table, values[0, 0], probes, weights.reshape(1, -1))


def solution(mesh):
    placed = (
        P(("group", "dp"), "mp", None, None),
        P(("group", "dp"), "mp", None),
        P(("group", "dp"), "mp", None),
        P(("group", "dp"), "mp"),
        P(("group", "dp")),
        P(("group", "mp"), "dp", None),
    )
    return jax.shard_map(
        functools.partial(body, mesh.shape["dp"], mesh.shape["mp"]),
        mesh=mesh, in_specs=placed, out_specs=P(("group", "mp"), "dp", None), check_vma=False
    )
```

```python
import functools

import jax
import jax.numpy as jnp
from jax import lax
from jax.experimental import pallas as pl
from jax.experimental.pallas import tpu as pltpu
from jax.sharding import PartitionSpec as P

BS = 64
STEPS = 32000.0
TINY = 1e-30
PITCH = 40
MESH = pl.DeviceIdType.MESH
BF16 = jnp.bfloat16
F32 = jnp.float32


def both_halves(x):
    low, high = x[:, :BS], x[:, BS:]
    return jnp.concatenate([low, low], axis=1), jnp.concatenate([high, high], axis=1)


def kernel(n_dp, n_mp, n_data, n_cells, slots,
           table, values_hbm, probes_hbm, weights, out,
           values, probes, flat, plain, turned, packed, gathered, wide_f32, wide, strips, psend, precv, csend, crecv, own_pred,
           wgather, total_back, ssend, srecv, own_sketch,
           local, gs, gr, ps, pr, cs, cr, ws, wr, ss, sr):
    dp, mp = lax.axis_index("dp"), lax.axis_index("mp")
    share = BS // n_dp
    owned = n_data // n_mp
    pairs = owned // 2
    depth = owned * BS
    half_cells = n_cells // 2
    hb = BS // 2
    side = lax.broadcasted_iota(jnp.int32, (hb, 2 * BS), 1) < BS

    probes_in = pltpu.make_async_copy(probes_hbm, probes, local.at[0])
    values_in = pltpu.make_async_copy(values_hbm, values, local.at[1])
    probes_in.start()
    values_in.start()

    barrier = pltpu.get_barrier_semaphore()
    for off in range(1, n_dp):
        pl.semaphore_signal(barrier, inc=1, device_id={"dp": lax.rem(dp + off, n_dp)}, device_id_type=MESH)
    for off in range(1, n_mp):
        pl.semaphore_signal(barrier, inc=1, device_id={"mp": lax.rem(mp + off, n_mp)}, device_id_type=MESH)

    def partner(x):
        return sum(lax.rem(mp // (1 << b) + (x >> b) % 2, 2) * (1 << b) for b in range(n_mp.bit_length() - 1))

    probes_in.wait()
    for c in range(half_cells):
        flat[c * share:(c + 1) * share] = jnp.concatenate([probes[c], probes[half_cells + c]], axis=1).astype(F32)
    packed[...] = flat[0:half_cells * share].astype(BF16)
    pl.semaphore_wait(barrier, n_dp + n_mp - 2)

    def remote(src, dst, send, recv, axis, peer):
        return pltpu.make_async_remote_copy(
            src_ref=src, dst_ref=dst, send_sem=send, recv_sem=recv,
            device_id={axis: peer}, device_id_type=MESH)

    for off in range(1, n_dp):
        remote(packed, gathered.at[off - 1], gs.at[off - 1], gr.at[off - 1],
               "dp", lax.rem(dp + off, n_dp)).start()

    values_in.wait()
    for q in range(hb):
        flat[pl.ds(q, slots, stride=PITCH), :] = values[:, q * 2 * BS:(q + 1) * 2 * BS].astype(F32)

    def turn(s, carry):
        for t in range(8):
            rows = flat[pl.ds(pl.multiple_of(s * (8 * PITCH) + t * PITCH, 8), hb), :]
            plain[s * 8 + t] = rows.astype(BF16)
            turned[s * 8 + t] = pltpu.roll(rows, BS, 1).astype(BF16)
        return carry

    lax.fori_loop(0, slots // 8, turn, 0)
    plain[slots] = jnp.zeros((hb, 2 * BS), BF16)
    turned[slots] = jnp.zeros((hb, 2 * BS), BF16)

    def build(block, carry):
        base = pl.multiple_of(block * BS, BS)
        for k in range(n_cells // 2):
            a = table[block * n_cells + 2 * k]
            b = table[block * n_cells + 2 * k + 1]
            lanes = slice(2 * k * BS, (2 * k + 2) * BS)
            strips[pl.ds(base, hb), lanes] = jnp.where(side, plain[a], turned[b])
            strips[pl.ds(base + hb, hb), lanes] = jnp.where(side, turned[a], plain[b])
        return carry

    def build_for(k):
        lax.fori_loop(0, owned, lambda b, carry: build(k * owned + b, carry), 0)

    peers = list(range(n_mp - 1, 0, -1))
    build_for(partner(peers[0]))

    def place(source, d):
        rows = source.astype(F32)
        start = pl.multiple_of(d * share, share)
        for c in range(half_cells):
            wide_f32[c, pl.ds(start, share), :] = rows[c * share:(c + 1) * share]

    place(packed[...], dp)
    for off in range(1, n_dp):
        remote(packed, gathered.at[off - 1], gs.at[off - 1], gr.at[off - 1], "dp", dp).wait_recv()
        place(gathered[off - 1], lax.rem(dp + n_dp - off, n_dp))
    for c in range(half_cells):
        low, high = both_halves(wide_f32[c])
        wide[c * BS:(c + 1) * BS] = low.astype(BF16)
        wide[(half_cells + c) * BS:(half_cells + c + 1) * BS] = high.astype(BF16)

    half = lax.broadcasted_iota(jnp.int32, (pairs * BS, 2 * BS), 1) < BS

    def rows_of(k):
        return pl.ds(pl.multiple_of(k * depth, depth), depth)

    def predict(peer):
        full = jnp.dot(strips[rows_of(peer), :], wide[...], preferred_element_type=F32)
        return jnp.where(half, full[:pairs * BS], full[pairs * BS:])

    for x in peers:
        if x != peers[0]:
            build_for(partner(x))
        pred = predict(partner(x))
        top = jnp.maximum(jnp.max(jnp.abs(pred), axis=0, keepdims=True), TINY)
        psend[x - 1] = jnp.round(pred * (STEPS / top)).astype(jnp.int32).astype(jnp.int16)
        csend[x - 1] = jnp.broadcast_to(top * (1.0 / STEPS), (8, 2 * BS))
        remote(csend.at[x - 1], crecv.at[x - 1], cs.at[x - 1], cr.at[x - 1], "mp", partner(x)).start()
        remote(psend.at[x - 1], precv.at[x - 1], ps.at[x - 1], pr.at[x - 1], "mp", partner(x)).start()
    build_for(mp)
    own_pred[...] = predict(mp)

    i0 = lax.broadcasted_iota(jnp.int32, (2 * BS, 2 * BS), 0)
    i1 = lax.broadcasted_iota(jnp.int32, (2 * BS, 2 * BS), 1)
    inner = lax.rem(i1, BS)
    origin = i1 - inner + 2 * lax.rem(inner, hb) + inner // hb
    order = (i0 == origin).astype(F32)
    mine = weights[:, pl.ds(pl.multiple_of(mp * depth, depth), depth)]
    sorted_w = jnp.concatenate(
        [jnp.dot(jnp.broadcast_to(mine[:, k * 2 * BS:(k + 1) * 2 * BS], (8, 2 * BS)), order,
                 precision=lax.Precision.HIGHEST, preferred_element_type=F32) for k in range(owned // 2)], axis=1)
    factor = jnp.concatenate(
        [jnp.broadcast_to(sorted_w[0:1, :pairs * BS], (BS, pairs * BS)),
         jnp.broadcast_to(sorted_w[0:1, pairs * BS:], (BS, pairs * BS))], axis=0)

    total = own_pred[...]
    for x in reversed(peers):
        remote(csend.at[x - 1], crecv.at[x - 1], cs.at[x - 1], cr.at[x - 1], "mp", mp).wait_recv()
        remote(psend.at[x - 1], precv.at[x - 1], ps.at[x - 1], pr.at[x - 1], "mp", mp).wait_recv()
        total = total + precv[x - 1].astype(jnp.int32).astype(F32) * crecv[x - 1, 0:1]
    wgather[0] = (factor * total.T).astype(BF16)
    for x in peers:
        remote(wgather.at[0], wgather.at[x], ws.at[x - 1], wr.at[x - 1], "mp", partner(x)).start()

    group = 8
    gp = group // 2
    cols = group * BS
    rows = gp * share

    def part_of(slot, k, g):
        chunk = wgather[slot]
        left = jnp.concatenate([chunk[:BS], chunk[BS:]], axis=1)
        return jnp.dot(left, strips[rows_of(k), g * cols:(g + 1) * cols], preferred_element_type=F32)

    n_groups = n_cells // group
    for off in range(n_mp):
        if off:
            remote(wgather.at[0], wgather.at[off], ws.at[off - 1], wr.at[off - 1], "mp", mp).wait_recv()
        for g in range(n_groups):
            lanes = slice(g * cols, (g + 1) * cols)
            part = part_of(off, partner(off) if off else mp, g)
            if off:
                part = part + total_back[:, lanes]
            if off < n_mp - 1:
                total_back[:, lanes] = part
                continue
            both = jnp.concatenate([part[:, :gp * BS], part[:, gp * BS:]], axis=0).T
            for d in range(n_dp):
                piece = jnp.concatenate(
                    [both[p * BS + d * share:p * BS + (d + 1) * share] for p in range(gp)], axis=0)
                ssend[d, g * rows:(g + 1) * rows] = piece.astype(BF16)

                @pl.when(dp == d)
                def _():
                    own_sketch[g * rows:(g + 1) * rows] = piece
            for o in range(1, n_dp):
                peer = lax.rem(dp + o, n_dp)
                remote(ssend.at[peer, pl.ds(g * rows, rows)], srecv.at[o - 1, pl.ds(g * rows, rows)],
                       ss.at[o - 1, g], sr.at[o - 1, g], "dp", peer).start()

    for g in range(n_groups):
        acc = own_sketch[g * rows:(g + 1) * rows]
        for off in range(1, n_dp):
            remote(ssend.at[0, pl.ds(g * rows, rows)], srecv.at[off - 1, pl.ds(g * rows, rows)],
                   ss.at[off - 1, g], sr.at[off - 1, g], "dp", dp).wait_recv()
            acc = acc + srecv[off - 1, g * rows:(g + 1) * rows].astype(F32)
        for p in range(gp):
            one = acc[p * share:(p + 1) * share]
            out[g * group + p] = one[:, :BS]
            out[g * group + gp + p] = one[:, BS:]

    for off in range(1, n_dp):
        remote(packed, gathered.at[off - 1], gs.at[off - 1], gr.at[off - 1], "dp", dp).wait_send()
        for g in range(n_groups):
            remote(ssend.at[0, pl.ds(g * rows, rows)], srecv.at[off - 1, pl.ds(g * rows, rows)],
                   ss.at[off - 1, g], sr.at[off - 1, g], "dp", dp).wait_send()
    for off in range(1, n_mp):
        remote(psend.at[off - 1], precv.at[off - 1], ps.at[off - 1], pr.at[off - 1], "mp", mp).wait_send()
        remote(csend.at[off - 1], crecv.at[off - 1], cs.at[off - 1], cr.at[off - 1], "mp", mp).wait_send()
        remote(wgather.at[0], wgather.at[off], ws.at[off - 1], wr.at[off - 1], "mp", mp).wait_send()


def body(n_dp, n_mp, values, rows, cols, counts, weights, probes):
    slots = values.shape[2]
    n_cells = probes.shape[0]
    share = probes.shape[1]
    n_data = weights.shape[0] // BS
    owned = n_data // n_mp
    pairs = owned // 2
    half_cells = n_cells // 2
    groups = n_cells // 8
    srows = 4 * share

    live = jnp.arange(slots, dtype=jnp.int32) < counts[0, 0]
    where = jnp.where(live, rows[0, 0] * n_cells + cols[0, 0], -1)
    places = jnp.arange(n_data * n_cells, dtype=jnp.int32)
    hit = places[:, None] == where[None, :]
    table = jnp.min(jnp.where(hit, jnp.arange(slots, dtype=jnp.int32)[None, :], slots), axis=1)

    vmem = pl.BlockSpec(memory_space=pltpu.VMEM)
    dma = pltpu.SemaphoreType.DMA
    return pl.pallas_call(
        functools.partial(kernel, n_dp, n_mp, n_data, n_cells, slots),
        out_shape=jax.ShapeDtypeStruct((n_cells, share, BS), F32),
        in_specs=[pl.BlockSpec(memory_space=pltpu.SMEM)] + [pl.BlockSpec(memory_space=pltpu.HBM)] * 2 + [vmem],
        out_specs=vmem,
        scratch_shapes=[
            pltpu.VMEM((slots, BS * BS), BF16),
            pltpu.VMEM((n_cells, share, BS), BF16),
            pltpu.VMEM((slots * PITCH, 2 * BS), F32),
            pltpu.VMEM((slots + 1, BS // 2, 2 * BS), BF16),
            pltpu.VMEM((slots + 1, BS // 2, 2 * BS), BF16),
            pltpu.VMEM((half_cells * share, 2 * BS), BF16),
            pltpu.VMEM((n_dp - 1, half_cells * share, 2 * BS), BF16),
            pltpu.VMEM((half_cells, BS, 2 * BS), F32),
            pltpu.VMEM((n_cells * BS, 2 * BS), BF16),
            pltpu.VMEM((n_data * BS, n_cells * BS), BF16),
            pltpu.VMEM((n_mp - 1, pairs * BS, 2 * BS), jnp.int16),
            pltpu.VMEM((n_mp - 1, pairs * BS, 2 * BS), jnp.int16),
            pltpu.VMEM((n_mp - 1, 8, 2 * BS), F32),
            pltpu.VMEM((n_mp - 1, 8, 2 * BS), F32),
            pltpu.VMEM((pairs * BS, 2 * BS), F32),
            pltpu.VMEM((n_mp, 2 * BS, pairs * BS), BF16),
            pltpu.VMEM((BS, n_cells * BS), F32),
            pltpu.VMEM((n_dp, groups * srows, 2 * BS), BF16),
            pltpu.VMEM((n_dp - 1, groups * srows, 2 * BS), BF16),
            pltpu.VMEM((groups * srows, 2 * BS), F32),
            dma((2,)),
            dma((n_dp - 1,)), dma((n_dp - 1,)),
            dma((n_mp - 1,)), dma((n_mp - 1,)),
            dma((n_mp - 1,)), dma((n_mp - 1,)),
            dma((n_mp - 1,)), dma((n_mp - 1,)),
            dma((n_dp - 1, groups)), dma((n_dp - 1, groups)),
        ],
        compiler_params=pltpu.CompilerParams(
            collective_id=0, has_side_effects=True, vmem_limit_bytes=48 * 1024 * 1024),
    )(table, values[0, 0], probes, weights.reshape(1, -1))


def solution(mesh):
    placed = (
        P(("group", "dp"), "mp", None, None),
        P(("group", "dp"), "mp", None),
        P(("group", "dp"), "mp", None),
        P(("group", "dp"), "mp"),
        P(("group", "dp")),
        P(("group", "mp"), "dp", None),
    )
    return jax.shard_map(
        functools.partial(body, mesh.shape["dp"], mesh.shape["mp"]),
        mesh=mesh, in_specs=placed, out_specs=P(("group", "mp"), "dp", None), check_vma=False
    )
```

```python
import functools

import jax
import jax.numpy as jnp
from jax import lax
from jax.experimental import pallas as pl
from jax.experimental.pallas import tpu as pltpu
from jax.sharding import PartitionSpec as P

BS = 64
STEPS = 32000.0
TINY = 1e-30
PITCH = 40
MESH = pl.DeviceIdType.MESH
BF16 = jnp.bfloat16
F32 = jnp.float32


def both_halves(x):
    low, high = x[:, :BS], x[:, BS:]
    return jnp.concatenate([low, low], axis=1), jnp.concatenate([high, high], axis=1)


def kernel(n_dp, n_mp, n_data, n_cells, slots,
           table, values_hbm, probes_hbm, weights, out,
           values, probes, flat, plain, turned, packed, gathered, wide_f32, wide, strips, psend, precv, csend, crecv, own_pred,
           wgather, total_back, ssend, srecv, own_sketch,
           local, gs, gr, ps, pr, cs, cr, ws, wr, ss, sr):
    dp, mp = lax.axis_index("dp"), lax.axis_index("mp")
    share = BS // n_dp
    owned = n_data // n_mp
    pairs = owned // 2
    depth = owned * BS
    half_cells = n_cells // 2
    hb = BS // 2
    side = lax.broadcasted_iota(jnp.int32, (hb, 2 * BS), 1) < BS

    probes_in = pltpu.make_async_copy(probes_hbm, probes, local.at[0])
    values_in = pltpu.make_async_copy(values_hbm, values, local.at[1])
    probes_in.start()
    values_in.start()

    barrier = pltpu.get_barrier_semaphore()
    for off in range(1, n_dp):
        pl.semaphore_signal(barrier, inc=1, device_id={"dp": lax.rem(dp + off, n_dp)}, device_id_type=MESH)
    for off in range(1, n_mp):
        pl.semaphore_signal(barrier, inc=1, device_id={"mp": lax.rem(mp + off, n_mp)}, device_id_type=MESH)

    def partner(x):
        return sum(lax.rem(mp // (1 << b) + (x >> b) % 2, 2) * (1 << b) for b in range(n_mp.bit_length() - 1))

    probes_in.wait()
    for c in range(half_cells):
        flat[c * share:(c + 1) * share] = jnp.concatenate([probes[c], probes[half_cells + c]], axis=1).astype(F32)
    packed[...] = flat[0:half_cells * share].astype(BF16)
    pl.semaphore_wait(barrier, n_dp + n_mp - 2)

    def remote(src, dst, send, recv, axis, peer):
        return pltpu.make_async_remote_copy(
            src_ref=src, dst_ref=dst, send_sem=send, recv_sem=recv,
            device_id={axis: peer}, device_id_type=MESH)

    for off in range(1, n_dp):
        remote(packed, gathered.at[off - 1], gs.at[off - 1], gr.at[off - 1],
               "dp", lax.rem(dp + off, n_dp)).start()

    values_in.wait()
    for q in range(hb):
        flat[pl.ds(q, slots, stride=PITCH), :] = values[:, q * 2 * BS:(q + 1) * 2 * BS].astype(F32)

    def turn(s, carry):
        for t in range(8):
            rows = flat[pl.ds(pl.multiple_of(s * (8 * PITCH) + t * PITCH, 8), hb), :]
            plain[s * 8 + t] = rows.astype(BF16)
            turned[s * 8 + t] = pltpu.roll(rows, BS, 1).astype(BF16)
        return carry

    lax.fori_loop(0, slots // 8, turn, 0)
    plain[slots] = jnp.zeros((hb, 2 * BS), BF16)
    turned[slots] = jnp.zeros((hb, 2 * BS), BF16)

    def build(block, carry):
        base = pl.multiple_of(block * BS, BS)
        for k in range(n_cells // 2):
            a = table[block * n_cells + 2 * k]
            b = table[block * n_cells + 2 * k + 1]
            lanes = slice(2 * k * BS, (2 * k + 2) * BS)
            strips[pl.ds(base, hb), lanes] = jnp.where(side, plain[a], turned[b])
            strips[pl.ds(base + hb, hb), lanes] = jnp.where(side, turned[a], plain[b])
        return carry

    lax.fori_loop(0, n_data, build, 0)
    peers = list(range(n_mp - 1, 0, -1))

    def place(source, d):
        rows = source.astype(F32)
        start = pl.multiple_of(d * share, share)
        for c in range(half_cells):
            wide_f32[c, pl.ds(start, share), :] = rows[c * share:(c + 1) * share]

    place(packed[...], dp)
    for off in range(1, n_dp):
        remote(packed, gathered.at[off - 1], gs.at[off - 1], gr.at[off - 1], "dp", dp).wait_recv()
        place(gathered[off - 1], lax.rem(dp + n_dp - off, n_dp))
    for c in range(half_cells):
        low, high = both_halves(wide_f32[c])
        wide[c * BS:(c + 1) * BS] = low.astype(BF16)
        wide[(half_cells + c) * BS:(half_cells + c + 1) * BS] = high.astype(BF16)

    half = lax.broadcasted_iota(jnp.int32, (pairs * BS, 2 * BS), 1) < BS

    def rows_of(k):
        return pl.ds(pl.multiple_of(k * depth, depth), depth)

    def predict(peer):
        full = jnp.dot(strips[rows_of(peer), :], wide[...], preferred_element_type=F32)
        return jnp.where(half, full[:pairs * BS], full[pairs * BS:])

    for x in peers:
        pred = predict(partner(x))
        top = jnp.maximum(jnp.max(jnp.abs(pred), axis=0, keepdims=True), TINY)
        psend[x - 1] = jnp.round(pred * (STEPS / top)).astype(jnp.int32).astype(jnp.int16)
        csend[x - 1] = jnp.broadcast_to(top * (1.0 / STEPS), (8, 2 * BS))
        remote(csend.at[x - 1], crecv.at[x - 1], cs.at[x - 1], cr.at[x - 1], "mp", partner(x)).start()
        remote(psend.at[x - 1], precv.at[x - 1], ps.at[x - 1], pr.at[x - 1], "mp", partner(x)).start()
    own_pred[...] = predict(mp)

    i0 = lax.broadcasted_iota(jnp.int32, (2 * BS, 2 * BS), 0)
    i1 = lax.broadcasted_iota(jnp.int32, (2 * BS, 2 * BS), 1)
    inner = lax.rem(i1, BS)
    origin = i1 - inner + 2 * lax.rem(inner, hb) + inner // hb
    order = (i0 == origin).astype(F32)
    mine = weights[:, pl.ds(pl.multiple_of(mp * depth, depth), depth)]
    sorted_w = jnp.concatenate(
        [jnp.dot(jnp.broadcast_to(mine[:, k * 2 * BS:(k + 1) * 2 * BS], (8, 2 * BS)), order,
                 precision=lax.Precision.HIGHEST, preferred_element_type=F32) for k in range(owned // 2)], axis=1)
    factor = jnp.concatenate(
        [jnp.broadcast_to(sorted_w[0:1, :pairs * BS], (BS, pairs * BS)),
         jnp.broadcast_to(sorted_w[0:1, pairs * BS:], (BS, pairs * BS))], axis=0)

    total = own_pred[...]
    for x in reversed(peers):
        remote(csend.at[x - 1], crecv.at[x - 1], cs.at[x - 1], cr.at[x - 1], "mp", mp).wait_recv()
        remote(psend.at[x - 1], precv.at[x - 1], ps.at[x - 1], pr.at[x - 1], "mp", mp).wait_recv()
        total = total + precv[x - 1].astype(jnp.int32).astype(F32) * crecv[x - 1, 0:1]
    wgather[0] = (factor * total.T).astype(BF16)
    for x in peers:
        remote(wgather.at[0], wgather.at[x], ws.at[x - 1], wr.at[x - 1], "mp", partner(x)).start()

    group = 8
    gp = group // 2
    cols = group * BS
    rows = gp * share

    def part_of(slot, k, g):
        chunk = wgather[slot]
        left = jnp.concatenate([chunk[:BS], chunk[BS:]], axis=1)
        return jnp.dot(left, strips[rows_of(k), g * cols:(g + 1) * cols], preferred_element_type=F32)

    n_groups = n_cells // group
    for off in range(n_mp):
        if off:
            remote(wgather.at[0], wgather.at[off], ws.at[off - 1], wr.at[off - 1], "mp", mp).wait_recv()
        for g in range(n_groups):
            lanes = slice(g * cols, (g + 1) * cols)
            part = part_of(off, partner(off) if off else mp, g)
            if off:
                part = part + total_back[:, lanes]
            if off < n_mp - 1:
                total_back[:, lanes] = part
                continue
            both = jnp.concatenate([part[:, :gp * BS], part[:, gp * BS:]], axis=0).T
            for d in range(n_dp):
                piece = jnp.concatenate(
                    [both[p * BS + d * share:p * BS + (d + 1) * share] for p in range(gp)], axis=0)
                ssend[d, g * rows:(g + 1) * rows] = piece.astype(BF16)
            own_sketch[g * gp * BS:(g + 1) * gp * BS] = both
            for o in range(1, n_dp):
                peer = lax.rem(dp + o, n_dp)
                remote(ssend.at[peer, pl.ds(g * rows, rows)], srecv.at[o - 1, pl.ds(g * rows, rows)],
                       ss.at[o - 1, g], sr.at[o - 1, g], "dp", peer).start()

    for g in range(n_groups):
        acc = jnp.concatenate(
            [own_sketch[pl.ds((g * gp + p) * BS + pl.multiple_of(dp * share, share), share), :] for p in range(gp)],
            axis=0)
        for off in range(1, n_dp):
            remote(ssend.at[0, pl.ds(g * rows, rows)], srecv.at[off - 1, pl.ds(g * rows, rows)],
                   ss.at[off - 1, g], sr.at[off - 1, g], "dp", dp).wait_recv()
            acc = acc + srecv[off - 1, g * rows:(g + 1) * rows].astype(F32)
        for p in range(gp):
            one = acc[p * share:(p + 1) * share]
            out[g * group + p] = one[:, :BS]
            out[g * group + gp + p] = one[:, BS:]

    for off in range(1, n_dp):
        remote(packed, gathered.at[off - 1], gs.at[off - 1], gr.at[off - 1], "dp", dp).wait_send()
        for g in range(n_groups):
            remote(ssend.at[0, pl.ds(g * rows, rows)], srecv.at[off - 1, pl.ds(g * rows, rows)],
                   ss.at[off - 1, g], sr.at[off - 1, g], "dp", dp).wait_send()
    for off in range(1, n_mp):
        remote(psend.at[off - 1], precv.at[off - 1], ps.at[off - 1], pr.at[off - 1], "mp", mp).wait_send()
        remote(csend.at[off - 1], crecv.at[off - 1], cs.at[off - 1], cr.at[off - 1], "mp", mp).wait_send()
        remote(wgather.at[0], wgather.at[off], ws.at[off - 1], wr.at[off - 1], "mp", mp).wait_send()


def body(n_dp, n_mp, values, rows, cols, counts, weights, probes):
    slots = values.shape[2]
    n_cells = probes.shape[0]
    share = probes.shape[1]
    n_data = weights.shape[0] // BS
    owned = n_data // n_mp
    pairs = owned // 2
    half_cells = n_cells // 2
    groups = n_cells // 8
    srows = 4 * share

    live = jnp.arange(slots, dtype=jnp.int32) < counts[0, 0]
    where = jnp.where(live, rows[0, 0] * n_cells + cols[0, 0], -1)
    places = jnp.arange(n_data * n_cells, dtype=jnp.int32)
    hit = places[:, None] == where[None, :]
    table = jnp.min(jnp.where(hit, jnp.arange(slots, dtype=jnp.int32)[None, :], slots), axis=1)

    vmem = pl.BlockSpec(memory_space=pltpu.VMEM)
    dma = pltpu.SemaphoreType.DMA
    return pl.pallas_call(
        functools.partial(kernel, n_dp, n_mp, n_data, n_cells, slots),
        out_shape=jax.ShapeDtypeStruct((n_cells, share, BS), F32),
        in_specs=[pl.BlockSpec(memory_space=pltpu.SMEM)] + [pl.BlockSpec(memory_space=pltpu.HBM)] * 2 + [vmem],
        out_specs=vmem,
        scratch_shapes=[
            pltpu.VMEM((slots, BS * BS), BF16),
            pltpu.VMEM((n_cells, share, BS), BF16),
            pltpu.VMEM((slots * PITCH, 2 * BS), F32),
            pltpu.VMEM((slots + 1, BS // 2, 2 * BS), BF16),
            pltpu.VMEM((slots + 1, BS // 2, 2 * BS), BF16),
            pltpu.VMEM((half_cells * share, 2 * BS), BF16),
            pltpu.VMEM((n_dp - 1, half_cells * share, 2 * BS), BF16),
            pltpu.VMEM((half_cells, BS, 2 * BS), F32),
            pltpu.VMEM((n_cells * BS, 2 * BS), BF16),
            pltpu.VMEM((n_data * BS, n_cells * BS), BF16),
            pltpu.VMEM((n_mp - 1, pairs * BS, 2 * BS), jnp.int16),
            pltpu.VMEM((n_mp - 1, pairs * BS, 2 * BS), jnp.int16),
            pltpu.VMEM((n_mp - 1, 8, 2 * BS), F32),
            pltpu.VMEM((n_mp - 1, 8, 2 * BS), F32),
            pltpu.VMEM((pairs * BS, 2 * BS), F32),
            pltpu.VMEM((n_mp, 2 * BS, pairs * BS), BF16),
            pltpu.VMEM((BS, n_cells * BS), F32),
            pltpu.VMEM((n_dp, groups * srows, 2 * BS), BF16),
            pltpu.VMEM((n_dp - 1, groups * srows, 2 * BS), BF16),
            pltpu.VMEM((half_cells * BS, 2 * BS), F32),
            dma((2,)),
            dma((n_dp - 1,)), dma((n_dp - 1,)),
            dma((n_mp - 1,)), dma((n_mp - 1,)),
            dma((n_mp - 1,)), dma((n_mp - 1,)),
            dma((n_mp - 1,)), dma((n_mp - 1,)),
            dma((n_dp - 1, groups)), dma((n_dp - 1, groups)),
        ],
        compiler_params=pltpu.CompilerParams(
            collective_id=0, has_side_effects=True, vmem_limit_bytes=60 * 1024 * 1024),
    )(table, values[0, 0], probes, weights.reshape(1, -1))


def solution(mesh):
    placed = (
        P(("group", "dp"), "mp", None, None),
        P(("group", "dp"), "mp", None),
        P(("group", "dp"), "mp", None),
        P(("group", "dp"), "mp"),
        P(("group", "dp")),
        P(("group", "mp"), "dp", None),
    )
    return jax.shard_map(
        functools.partial(body, mesh.shape["dp"], mesh.shape["mp"]),
        mesh=mesh, in_specs=placed, out_specs=P(("group", "mp"), "dp", None), check_vma=False
    )
```

```python
import functools

import jax
import jax.numpy as jnp
from jax import lax
from jax.experimental import pallas as pl
from jax.experimental.pallas import tpu as pltpu
from jax.sharding import PartitionSpec as P

BS = 64
STEPS = 32000.0
TINY = 1e-30
PITCH = 40
MESH = pl.DeviceIdType.MESH
BF16 = jnp.bfloat16
F32 = jnp.float32


def both_halves(x):
    low, high = x[:, :BS], x[:, BS:]
    return jnp.concatenate([low, low], axis=1), jnp.concatenate([high, high], axis=1)


def kernel(n_dp, n_mp, n_data, n_cells, slots,
           table, values_hbm, probes_hbm, weights, out,
           values, probes, flat, plain, turned, packed, gathered, wide_f32, wide, strips, psend, precv, csend, crecv, own_pred,
           wgather, total_back, ssend, srecv, own_sketch,
           local, gs, gr, ps, pr, cs, cr, ws, wr, ss, sr):
    dp, mp = lax.axis_index("dp"), lax.axis_index("mp")
    share = BS // n_dp
    owned = n_data // n_mp
    pairs = owned // 2
    depth = owned * BS
    half_cells = n_cells // 2
    hb = BS // 2
    side = lax.broadcasted_iota(jnp.int32, (hb, 2 * BS), 1) < BS

    probes_in = pltpu.make_async_copy(probes_hbm, probes, local.at[0])
    values_in = pltpu.make_async_copy(values_hbm, values, local.at[1])
    probes_in.start()
    values_in.start()

    barrier = pltpu.get_barrier_semaphore()
    for off in range(1, n_dp):
        pl.semaphore_signal(barrier, inc=1, device_id={"dp": lax.rem(dp + off, n_dp)}, device_id_type=MESH)
    for off in range(1, n_mp):
        pl.semaphore_signal(barrier, inc=1, device_id={"mp": lax.rem(mp + off, n_mp)}, device_id_type=MESH)

    def partner(x):
        return sum(lax.rem(mp // (1 << b) + (x >> b) % 2, 2) * (1 << b) for b in range(n_mp.bit_length() - 1))

    probes_in.wait()
    for c in range(half_cells):
        flat[c * share:(c + 1) * share] = jnp.concatenate([probes[c], probes[half_cells + c]], axis=1).astype(F32)
    packed[...] = flat[0:half_cells * share].astype(BF16)
    pl.semaphore_wait(barrier, n_dp + n_mp - 2)

    def remote(src, dst, send, recv, axis, peer):
        return pltpu.make_async_remote_copy(
            src_ref=src, dst_ref=dst, send_sem=send, recv_sem=recv,
            device_id={axis: peer}, device_id_type=MESH)

    for off in range(1, n_dp):
        remote(packed, gathered.at[off - 1], gs.at[off - 1], gr.at[off - 1],
               "dp", lax.rem(dp + off, n_dp)).start()

    values_in.wait()
    for q in range(hb):
        flat[pl.ds(q, slots, stride=PITCH), :] = values[:, q * 2 * BS:(q + 1) * 2 * BS].astype(F32)

    def turn(s, carry):
        for t in range(8):
            rows = flat[pl.ds(pl.multiple_of(s * (8 * PITCH) + t * PITCH, 8), hb), :]
            plain[s * 8 + t] = rows.astype(BF16)
            turned[s * 8 + t] = pltpu.roll(rows, BS, 1).astype(BF16)
        return carry

    lax.fori_loop(0, slots // 8, turn, 0)
    plain[slots] = jnp.zeros((hb, 2 * BS), BF16)
    turned[slots] = jnp.zeros((hb, 2 * BS), BF16)

    def build(block, carry):
        base = pl.multiple_of(block * BS, BS)
        for k in range(n_cells // 2):
            a = table[block * n_cells + 2 * k]
            b = table[block * n_cells + 2 * k + 1]
            lanes = slice(2 * k * BS, (2 * k + 2) * BS)
            strips[pl.ds(base, hb), lanes] = jnp.where(side, plain[a], turned[b])
            strips[pl.ds(base + hb, hb), lanes] = jnp.where(side, turned[a], plain[b])
        return carry

    lax.fori_loop(0, n_data, build, 0)
    peers = list(range(n_mp - 1, 0, -1))

    def place(source, d):
        rows = source.astype(F32)
        start = pl.multiple_of(d * share, share)
        for c in range(half_cells):
            wide_f32[c, pl.ds(start, share), :] = rows[c * share:(c + 1) * share]

    place(packed[...], dp)
    for off in range(1, n_dp):
        remote(packed, gathered.at[off - 1], gs.at[off - 1], gr.at[off - 1], "dp", dp).wait_recv()
        place(gathered[off - 1], lax.rem(dp + n_dp - off, n_dp))
    for c in range(half_cells):
        low, high = both_halves(wide_f32[c])
        wide[c * BS:(c + 1) * BS] = low.astype(BF16)
        wide[(half_cells + c) * BS:(half_cells + c + 1) * BS] = high.astype(BF16)

    half = lax.broadcasted_iota(jnp.int32, (pairs * BS, 2 * BS), 1) < BS

    def rows_of(k):
        return pl.ds(pl.multiple_of(k * depth, depth), depth)

    def predict(peer):
        full = jnp.dot(strips[rows_of(peer), :], wide[...], preferred_element_type=F32)
        return jnp.where(half, full[:pairs * BS], full[pairs * BS:])

    for x in peers:
        pred = predict(partner(x))
        top = jnp.maximum(jnp.max(jnp.abs(pred), axis=0, keepdims=True), TINY)
        psend[x - 1] = jnp.round(pred * (STEPS / top)).astype(jnp.int32).astype(jnp.int16)
        csend[x - 1] = jnp.broadcast_to(top * (1.0 / STEPS), (8, 2 * BS))
        remote(csend.at[x - 1], crecv.at[x - 1], cs.at[x - 1], cr.at[x - 1], "mp", partner(x)).start()
        remote(psend.at[x - 1], precv.at[x - 1], ps.at[x - 1], pr.at[x - 1], "mp", partner(x)).start()
    own_pred[...] = predict(mp)

    i0 = lax.broadcasted_iota(jnp.int32, (2 * BS, 2 * BS), 0)
    i1 = lax.broadcasted_iota(jnp.int32, (2 * BS, 2 * BS), 1)
    inner = lax.rem(i1, BS)
    origin = i1 - inner + 2 * lax.rem(inner, hb) + inner // hb
    order = (i0 == origin).astype(F32)
    mine = weights[:, pl.ds(pl.multiple_of(mp * depth, depth), depth)]
    sorted_w = jnp.concatenate(
        [jnp.dot(jnp.broadcast_to(mine[:, k * 2 * BS:(k + 1) * 2 * BS], (8, 2 * BS)), order,
                 precision=lax.Precision.HIGHEST, preferred_element_type=F32) for k in range(owned // 2)], axis=1)
    factor = jnp.concatenate(
        [jnp.broadcast_to(sorted_w[0:1, :pairs * BS], (BS, pairs * BS)),
         jnp.broadcast_to(sorted_w[0:1, pairs * BS:], (BS, pairs * BS))], axis=0)

    total = own_pred[...]
    for x in reversed(peers):
        remote(csend.at[x - 1], crecv.at[x - 1], cs.at[x - 1], cr.at[x - 1], "mp", mp).wait_recv()
        remote(psend.at[x - 1], precv.at[x - 1], ps.at[x - 1], pr.at[x - 1], "mp", mp).wait_recv()
        total = total + precv[x - 1].astype(jnp.int32).astype(F32) * crecv[x - 1, 0:1]
    wgather[0] = (factor * total.T).astype(BF16)
    for x in peers:
        remote(wgather.at[0], wgather.at[x], ws.at[x - 1], wr.at[x - 1], "mp", partner(x)).start()

    group = 8
    gp = group // 2
    cols = group * BS
    rows = gp * share

    def part_of(slot, k, g):
        chunk = wgather[slot]
        left = jnp.concatenate([chunk[:BS], chunk[BS:]], axis=1)
        return jnp.dot(left, strips[rows_of(k), g * cols:(g + 1) * cols], preferred_element_type=F32)

    n_groups = n_cells // group
    for step, off in enumerate([0] + peers):
        if off:
            remote(wgather.at[0], wgather.at[off], ws.at[off - 1], wr.at[off - 1], "mp", mp).wait_recv()
        for g in range(n_groups):
            lanes = slice(g * cols, (g + 1) * cols)
            part = part_of(off, partner(off) if off else mp, g)
            if off:
                part = part + total_back[:, lanes]
            if step < n_mp - 1:
                total_back[:, lanes] = part
                continue
            both = jnp.concatenate([part[:, :gp * BS], part[:, gp * BS:]], axis=0).T
            for d in range(n_dp):
                piece = jnp.concatenate(
                    [both[p * BS + d * share:p * BS + (d + 1) * share] for p in range(gp)], axis=0)
                ssend[d, g * rows:(g + 1) * rows] = piece.astype(BF16)
            own_sketch[g * gp * BS:(g + 1) * gp * BS] = both
            for o in range(1, n_dp):
                peer = lax.rem(dp + o, n_dp)
                remote(ssend.at[peer, pl.ds(g * rows, rows)], srecv.at[o - 1, pl.ds(g * rows, rows)],
                       ss.at[o - 1, g], sr.at[o - 1, g], "dp", peer).start()

    for g in range(n_groups):
        acc = jnp.concatenate(
            [own_sketch[pl.ds((g * gp + p) * BS + pl.multiple_of(dp * share, share), share), :] for p in range(gp)],
            axis=0)
        for off in range(1, n_dp):
            remote(ssend.at[0, pl.ds(g * rows, rows)], srecv.at[off - 1, pl.ds(g * rows, rows)],
                   ss.at[off - 1, g], sr.at[off - 1, g], "dp", dp).wait_recv()
            acc = acc + srecv[off - 1, g * rows:(g + 1) * rows].astype(F32)
        for p in range(gp):
            one = acc[p * share:(p + 1) * share]
            out[g * group + p] = one[:, :BS]
            out[g * group + gp + p] = one[:, BS:]

    for off in range(1, n_dp):
        remote(packed, gathered.at[off - 1], gs.at[off - 1], gr.at[off - 1], "dp", dp).wait_send()
        for g in range(n_groups):
            remote(ssend.at[0, pl.ds(g * rows, rows)], srecv.at[off - 1, pl.ds(g * rows, rows)],
                   ss.at[off - 1, g], sr.at[off - 1, g], "dp", dp).wait_send()
    for off in range(1, n_mp):
        remote(psend.at[off - 1], precv.at[off - 1], ps.at[off - 1], pr.at[off - 1], "mp", mp).wait_send()
        remote(csend.at[off - 1], crecv.at[off - 1], cs.at[off - 1], cr.at[off - 1], "mp", mp).wait_send()
        remote(wgather.at[0], wgather.at[off], ws.at[off - 1], wr.at[off - 1], "mp", mp).wait_send()


def body(n_dp, n_mp, values, rows, cols, counts, weights, probes):
    slots = values.shape[2]
    n_cells = probes.shape[0]
    share = probes.shape[1]
    n_data = weights.shape[0] // BS
    owned = n_data // n_mp
    pairs = owned // 2
    half_cells = n_cells // 2
    groups = n_cells // 8
    srows = 4 * share

    live = jnp.arange(slots, dtype=jnp.int32) < counts[0, 0]
    where = jnp.where(live, rows[0, 0] * n_cells + cols[0, 0], -1)
    places = jnp.arange(n_data * n_cells, dtype=jnp.int32)
    hit = places[:, None] == where[None, :]
    table = jnp.min(jnp.where(hit, jnp.arange(slots, dtype=jnp.int32)[None, :], slots), axis=1)

    vmem = pl.BlockSpec(memory_space=pltpu.VMEM)
    dma = pltpu.SemaphoreType.DMA
    return pl.pallas_call(
        functools.partial(kernel, n_dp, n_mp, n_data, n_cells, slots),
        out_shape=jax.ShapeDtypeStruct((n_cells, share, BS), F32),
        in_specs=[pl.BlockSpec(memory_space=pltpu.SMEM)] + [pl.BlockSpec(memory_space=pltpu.HBM)] * 2 + [vmem],
        out_specs=vmem,
        scratch_shapes=[
            pltpu.VMEM((slots, BS * BS), BF16),
            pltpu.VMEM((n_cells, share, BS), BF16),
            pltpu.VMEM((slots * PITCH, 2 * BS), F32),
            pltpu.VMEM((slots + 1, BS // 2, 2 * BS), BF16),
            pltpu.VMEM((slots + 1, BS // 2, 2 * BS), BF16),
            pltpu.VMEM((half_cells * share, 2 * BS), BF16),
            pltpu.VMEM((n_dp - 1, half_cells * share, 2 * BS), BF16),
            pltpu.VMEM((half_cells, BS, 2 * BS), F32),
            pltpu.VMEM((n_cells * BS, 2 * BS), BF16),
            pltpu.VMEM((n_data * BS, n_cells * BS), BF16),
            pltpu.VMEM((n_mp - 1, pairs * BS, 2 * BS), jnp.int16),
            pltpu.VMEM((n_mp - 1, pairs * BS, 2 * BS), jnp.int16),
            pltpu.VMEM((n_mp - 1, 8, 2 * BS), F32),
            pltpu.VMEM((n_mp - 1, 8, 2 * BS), F32),
            pltpu.VMEM((pairs * BS, 2 * BS), F32),
            pltpu.VMEM((n_mp, 2 * BS, pairs * BS), BF16),
            pltpu.VMEM((BS, n_cells * BS), F32),
            pltpu.VMEM((n_dp, groups * srows, 2 * BS), BF16),
            pltpu.VMEM((n_dp - 1, groups * srows, 2 * BS), BF16),
            pltpu.VMEM((half_cells * BS, 2 * BS), F32),
            dma((2,)),
            dma((n_dp - 1,)), dma((n_dp - 1,)),
            dma((n_mp - 1,)), dma((n_mp - 1,)),
            dma((n_mp - 1,)), dma((n_mp - 1,)),
            dma((n_mp - 1,)), dma((n_mp - 1,)),
            dma((n_dp - 1, groups)), dma((n_dp - 1, groups)),
        ],
        compiler_params=pltpu.CompilerParams(
            collective_id=0, has_side_effects=True, vmem_limit_bytes=60 * 1024 * 1024),
    )(table, values[0, 0], probes, weights.reshape(1, -1))


def solution(mesh):
    placed = (
        P(("group", "dp"), "mp", None, None),
        P(("group", "dp"), "mp", None),
        P(("group", "dp"), "mp", None),
        P(("group", "dp"), "mp"),
        P(("group", "dp")),
        P(("group", "mp"), "dp", None),
    )
    return jax.shard_map(
        functools.partial(body, mesh.shape["dp"], mesh.shape["mp"]),
        mesh=mesh, in_specs=placed, out_specs=P(("group", "mp"), "dp", None), check_vma=False
    )
```
